32 devices in a mesh: grp: 4 (over x, core), box: 8 (over z, y).
Axes of the slice: x: 2, y: 2, z: 4, core: 2. Of those that a mesh axis runs over, the one named last changes fastest.
Arguments:
- source_field: float32 [128, 256, 128], P('grp', 'box'), may hold values from -7 to 7
- region_tags: int32 [128, 256, 128], P('grp', 'box'), may hold values from 0 to 7
- region_coef: float32 [8], replicated, may hold values from 0.2 to 5
- roughness: float32 [128, 256, 128], P('grp', 'box'), may hold values from 0.5 to 2
Outputs:
- solution: float32 [128, 256, 128], P('grp', 'box')
- residual: float32 [128, 256, 128], P('grp', 'box')
The draws below stay inside these ranges and needn't reach their ends.
All inputs are finite; a program needn't handle non-finite values.
Results may differ from the reference program's by a relative error of at most 0.0003.
Values sent between devices are 32-bit elements; how exact they have to be, the bound alone decides.
A program may use at most 192 MiB of HBM per device.

```python
import math
import jax
import jax.numpy as jnp

LEVELS = 5
NU = 2
NB = 4
CYCLES = 2
REGIONS = 8
NX = 128
NY = 256
NZ = 128


def draw_source_field(key, part):
    pos_x = (jnp.arange(NX, dtype=jnp.float32) + 0.5) / NX
    pos_y = (jnp.arange(NY, dtype=jnp.float32) + 0.5) / NY
    pos_z = (jnp.arange(NZ, dtype=jnp.float32) + 0.5) / NZ
    rough = jnp.clip(jax.random.normal(key, (NX, NY, NZ), jnp.float32), -6.0, 6.0)
    bump = jnp.sin(math.pi * pos_x)[:, None, None] * jnp.sin(math.pi * pos_y)[None, :, None] * jnp.sin(math.pi * pos_z)[None, None, :]
    return rough + 0.5 * bump


def plant(values, stream_key, low, high):
    extent = values.shape
    spot = [jax.random.randint(jax.random.fold_in(stream_key, axis), (), 0, extent[axis]) for axis in range(len(extent))]
    values = values.at[tuple(spot)].set(low)
    longest = extent.index(max(extent))
    spot[longest] = (spot[longest] + 1) % extent[longest]
    return values.at[tuple(spot)].set(high)


def levels(key, extent, shards, smallest, top_value):
    level = 1.0
    for axis_at, shards_of in shards:
        heights = jax.random.uniform(jax.random.fold_in(jax.random.fold_in(key, 6), axis_at), (shards_of,), jnp.float32, smallest / len(shards), top_value / len(shards))
        level = level * jnp.repeat(jnp.exp(heights), extent[axis_at] // shards_of).reshape((-1,) + (1,) * (len(extent) - 1 - axis_at))
    return level


def setup_inputs(seed: int = 0) -> dict:
    key_list = jax.random.split(jax.random.key(seed), 5)
    source_field = draw_source_field(jax.random.fold_in(key_list[4], 71), 0)
    region_tags = plant(jax.random.randint(key_list[1], (NX, NY, NZ), 0, REGIONS), jax.random.fold_in(key_list[1], 1), 0, REGIONS - 1).astype(jnp.int32)
    region_coef = jnp.clip(jnp.exp(jax.random.uniform(key_list[2], (REGIONS,), jnp.float32, math.log(0.2), math.log(5.0))), 0.2, 5.0)
    roughness = jnp.clip(jnp.exp(math.log(2.0) - 1.3862944 * jax.random.uniform(key_list[3], (NX, NY, NZ), jnp.float32) ** levels(key_list[3], (NX, NY, NZ), ((0, 4), (1, 8)), -0.2, 0.2)), 0.5, 2.0)
    return {"source_field": source_field, "region_tags": region_tags, "region_coef": region_coef, "roughness": roughness}


relax_weight = 0.8


def coarsen(values):
    size_x, size_y, size_z = values.shape
    return values.reshape(size_x // 2, 2, size_y // 2, 2, size_z // 2, 2).sum(axis=(1, 3, 5))


def refine(values):
    return jnp.repeat(jnp.repeat(jnp.repeat(values, 2, 0), 2, 1), 2, 2)


def neighbours(padded):
    return [padded[2:, 1:-1, 1:-1], padded[:-2, 1:-1, 1:-1], padded[1:-1, 2:, 1:-1],
            padded[1:-1, :-2, 1:-1], padded[1:-1, 1:-1, 2:], padded[1:-1, 1:-1, :-2]]


def weights_of(coef_padded):
    center = coef_padded[1:-1, 1:-1, 1:-1]
    face_weights = [(center + other) * 0.5 for other in neighbours(coef_padded)]
    diag_sum = face_weights[0]
    for other in face_weights[1:]:
        diag_sum = diag_sum + other
    return face_weights, diag_sum


def apply_op(values, face_weights, diag_sum):
    near = neighbours(jnp.pad(values, 1))
    total = face_weights[0] * near[0]
    for index in range(1, 6):
        total = total + face_weights[index] * near[index]
    return diag_sum * values - total


def smooth(values, source, face_weights, diag_sum, count):
    for sweep_index in range(count):
        values = values + relax_weight * (source - apply_op(values, face_weights, diag_sum)) / diag_sum
    return values


def krylov_solve(source, face_weights, diag_sum):
    values = jnp.zeros_like(source)
    remain = source
    direction = source
    norm_now = jnp.sum(remain * remain)
    for step_index in range(NB):
        image = apply_op(direction, face_weights, diag_sum)
        alpha = norm_now / jnp.sum(direction * image)
        values = values + alpha * direction
        remain = remain - alpha * image
        norm_next = jnp.sum(remain * remain)
        direction = remain + (norm_next / norm_now) * direction
        norm_now = norm_next
    return values


def v_cycle(level_index, values, source, operators):
    face_weights, diag_sum = operators[level_index]
    if level_index == LEVELS - 1:
        return krylov_solve(source, face_weights, diag_sum)
    values = smooth(values, source, face_weights, diag_sum, NU)
    remain = source - apply_op(values, face_weights, diag_sum)
    coarse_source = 0.5 * coarsen(remain)
    correction = v_cycle(level_index + 1, jnp.zeros_like(coarse_source), coarse_source, operators)
    values = values + refine(correction)
    return smooth(values, source, face_weights, diag_sum, NU)


def reference(source_field, region_tags, region_coef, roughness):
    coefficient = region_coef[region_tags] * roughness
    fields = [coefficient]
    for level_index in range(1, LEVELS):
        fields.append(coarsen(fields[-1]) * 0.125)
    operators = [weights_of(jnp.pad(field, 1)) for field in fields]
    solution = jnp.zeros_like(source_field)
    for cycle_index in range(CYCLES):
        solution = v_cycle(0, solution, source_field, operators)
    residual = source_field - apply_op(solution, operators[0][0], operators[0][1])
    return solution, residual
```

```python
import functools
import jax
import jax.numpy as jnp
from jax import lax
from jax.experimental import pallas as pl
from jax.experimental.pallas import tpu as pltpu
from jax.sharding import PartitionSpec as P

NB = 4
LANES = 128
HX = 8
YO = 16
GX = 4
GY = 8
DIRECTIONS = [(dx, dy) for dx in (-1, 0, 1) for dy in (-1, 0, 1) if (dx, dy) != (0, 0)]


class Level:
    def __init__(self, shift, nx, ny, x0, y0, ylo, yhi, refs):
        self.shift, self.nx, self.ny, self.x0, self.y0 = shift, nx, ny, x0, y0
        self.ylo, self.yhi = ylo, yhi
        self.C, self.WL, self.WH, self.G, self.D, self.VA, self.VB = refs


def lane_index(shape):
    return lax.broadcasted_iota(jnp.int32, shape, len(shape) - 1)


def roll(values, shift):
    return pltpu.roll(values, shift % LANES, values.ndim - 1)


def pair_sum(values, shift):
    even = (lane_index(values.shape) // shift) % 2 == 0
    return values + jnp.where(even, roll(values, LANES - shift), roll(values, shift))


def off_diagonal(L, V, x, n, y, rows):
    block = V[pl.ds(x - 1, n + 2), pl.ds(y, rows), :]
    coef = L.C[pl.ds(x - 1, n + 2), pl.ds(y, rows), :]
    flow = block * coef
    center, near = block[1:-1], coef[1:-1]
    v_down = V[pl.ds(x, n), pl.ds(y - 1, rows), :]
    v_up = V[pl.ds(x, n), pl.ds(y + 1, rows), :]
    c_down = L.C[pl.ds(x, n), pl.ds(y - 1, rows), :]
    c_up = L.C[pl.ds(x, n), pl.ds(y + 1, rows), :]
    total = (block[:-2] + block[2:]) + (v_down + v_up)
    total = near * total + (flow[:-2] + flow[2:]) + (c_down * v_down + c_up * v_up)
    total = total + L.WL[pl.ds(x, n), pl.ds(y, rows), :] * roll(center, L.shift)
    total = total + L.WH[pl.ds(x, n), pl.ds(y, rows), :] * roll(center, LANES - L.shift)
    return center, total


def each_x(start, count, step, body):
    def run(i, carry):
        body(start + i * step, i)
        return carry

    lax.fori_loop(0, count // step, run, 0)


def tiles(lo, hi):
    return range(lo, hi, 8)


def operators(L, k):
    def body(x, i):
        for y in tiles(L.ylo, L.yhi):
            at = (pl.ds(x, 2), pl.ds(y, 8), slice(None))
            coef = L.C[pl.ds(x - 1, 4), pl.ds(y, 8), :]
            c = coef[1:-1]
            lane = lane_index(c.shape)
            down = jnp.where(lane < L.shift, 0.0, roll(c, L.shift))
            up = jnp.where(lane >= LANES - L.shift, 0.0, roll(c, LANES - L.shift))
            L.WL[at] = jnp.where(lane < L.shift, 0.0, c + down)
            L.WH[at] = jnp.where(lane >= LANES - L.shift, 0.0, c + up)
            diag = 6.0 * c + (coef[:-2] + coef[2:]) + (down + up)
            diag = diag + (L.C[pl.ds(x, 2), pl.ds(y - 1, 8), :] + L.C[pl.ds(x, 2), pl.ds(y + 1, 8), :])
            L.D[at] = diag
            L.G[at] = jnp.where(c > 0.0, 0.8 / jnp.where(c > 0.0, diag, 1.0), 0.0)

    each_x(L.x0 - k, L.nx + 2 * k, 2, body)


def first_sweep(L, F, dst, k):
    def body(x, i):
        for y in tiles(L.ylo, L.yhi):
            at = (pl.ds(x, 2), pl.ds(y, 8), slice(None))
            dst[at] = L.G[at] * F[at]

    each_x(L.x0 - k, L.nx + 2 * k, 2, body)


def sweep(L, F, src, dst, k):
    def body(x, i):
        for y in tiles(L.ylo, L.yhi):
            at = (pl.ds(x, 2), pl.ds(y, 8), slice(None))
            center, total = off_diagonal(L, src, x, 2, y, 8)
            dst[at] = 0.2 * center + L.G[at] * (F[at] + total)

    each_x(L.x0 - k, L.nx + 2 * k, 2, body)


def residual_pairs(L, F, V, R):
    def body(x, i):
        for y in tiles(L.y0, L.y0 + L.ny):
            at = (pl.ds(x, 2), pl.ds(y, 8), slice(None))
            center, total = off_diagonal(L, V, x, 2, y, 8)
            left = F[at] - L.D[at] * center + total
            R[i, pl.ds(y - L.y0, 8), :] = left[0] + left[1]

    each_x(L.x0, L.nx, 2, body)


def coef_pairs(L, R):
    def body(x, i):
        for y in tiles(L.y0, L.y0 + L.ny):
            c = L.C[pl.ds(x, 2), pl.ds(y, 8), :]
            R[i, pl.ds(y - L.y0, 8), :] = c[0] + c[1]

    each_x(L.x0, L.nx, 2, body)


def coarse_row(L, R, i, factor):
    half = L.ny // 2
    rows = R[i, pl.ds(0, half, stride=2), :] + R[i, pl.ds(1, half, stride=2), :]
    return pair_sum(rows, L.shift) * factor


def coarse_rows(L, R, factor, dst, x0, y0):
    def body(i, _):
        dst[x0 + i, pl.ds(y0, L.ny // 2), :] = coarse_row(L, R, i, factor)

    each_x(0, L.nx // 2, 1, body)


def packed(L, R, factor):
    count = L.nx // 2
    rows = [coarse_row(L, R, i, factor) for i in range(count)]
    which = lane_index(rows[0].shape) % count
    out = rows[0]
    for i in range(1, count):
        out = jnp.where(which == i, rows[i], out)
    return out


def unpack(slots, flat, dst, ng, nb, tx, ty):
    def body(g, _):
        for b in range(nb):
            flat[pl.ds(b * ty, ty), :] = slots[g * nb + b]
        for y in tiles(0, nb * ty):
            rows = flat[pl.ds(y, 8), :]
            rolled = {d: roll(rows, d) for d in range(1 - tx, tx)}
            which = lane_index(rows.shape) % tx
            for i in range(tx):
                out = rolled[-i]
                for d in range(1, tx):
                    out = jnp.where(which == d, rolled[d - i], out)
                dst[GX + g * tx + i, pl.ds(GY + y, 8), :] = out

    each_x(0, ng, 1, body)


def add_refined(L, src, dst, E, ex, ey, k):
    half = (L.yhi - L.ylo) // 2

    def body(x, i):
        e = E[ex + i, pl.ds(ey, half), :]
        for dx in range(2):
            for phase in range(2):
                at = (x + dx, pl.ds(L.ylo + phase, half, stride=2), slice(None))
                dst[at] = src[at] + e

    each_x(L.x0 - k, L.nx + 2 * k, 2, body)


def total_of(values):
    return jnp.sum(values, axis=(0, 1, 2), keepdims=True)


def krylov(L, F, E, V):
    at = (pl.ds(L.x0, L.nx), pl.ds(L.y0, L.ny), slice(None))
    remain = F[at]
    direction = remain
    values = jnp.zeros_like(remain)
    norm_now = total_of(remain * remain)
    for step in range(NB):
        V[at] = direction
        _, total = off_diagonal(L, V, L.x0, L.nx, L.y0, L.ny)
        image = L.D[at] * direction - total
        alpha = norm_now / total_of(direction * image)
        values = values + alpha * direction
        if step < NB - 1:
            remain = remain - alpha * image
            norm_next = total_of(remain * remain)
            direction = remain + (norm_next / norm_now) * direction
            norm_now = norm_next
    E[at] = values


def zero(ref):
    def body(i, _):
        ref[i] = jnp.zeros(ref.shape[1:], ref.dtype)

    each_x(0, ref.shape[0], 1, body)


def kernel(ng, nb, source, tags, coef, rough, out_v, out_r, *scratch):
    scratch = list(scratch)

    def take(count):
        taken = scratch[:count]
        del scratch[:count]
        return taken

    nx, ny = source.shape[0], source.shape[1]
    L = []
    for l in range(3):
        L.append(Level(1 << l, nx >> l, ny >> l, HX, YO, 8, (ny >> l) + 24, take(7)))
    tx, ty = nx >> 3, ny >> 3
    L.append(Level(8, ng * tx, nb * ty, GX, GY, GY, GY + nb * ty, take(7)))
    L.append(Level(16, ng * tx // 2, nb * ty // 2, 2, GY, GY, GY + nb * ty // 2, take(7)))
    f0, f1a, f1b, f2a, f2b, f3, f4, kept = take(8)
    f1, f2 = (f1a, f1b), (f2a, f2b)
    R0, R1, R2, R3, flat = take(5)
    slots = take(3)
    halo_send, halo_recv, all_send, all_recv = take(4)

    g, b = lax.axis_index("grp"), lax.axis_index("box")
    me = g * nb + b
    count = ng * nb

    for ref in [f0, f1a, f1b, f2a, f2b, kept]:
        zero(ref)
    for level in L:
        zero(level.C)
        zero(level.VA)
        zero(level.VB)

    barrier = pltpu.get_barrier_semaphore()

    def others(body):
        def run(i, carry):
            other = lax.rem(me + i, count)
            body(other // nb, lax.rem(other, nb))
            return carry

        lax.fori_loop(1, count, run, 0)

    others(lambda go, bo: pl.semaphore_signal(
        barrier, inc=1, device_id=(go, bo), device_id_type=pl.DeviceIdType.MESH))

    def halo_copies(ref, level, h, slot):
        for index, (dx, dy) in enumerate(DIRECTIONS):
            n, m = level.nx, level.ny
            sx, tx_, wx = {-1: (HX, HX + n, h), 0: (HX, HX, n), 1: (HX + n - h, HX - h, h)}[dx]
            sy, ty_, wy = {-1: (YO, YO + m, 8), 0: (YO, YO, m), 1: (YO + m - 8, YO - 8, 8)}[dy]
            to_g, to_b, from_g, from_b = g + dx, b + dy, g - dx, b - dy
            sends = (to_g >= 0) & (to_g < ng) & (to_b >= 0) & (to_b < nb)
            receives = (from_g >= 0) & (from_g < ng) & (from_b >= 0) & (from_b < nb)
            copy = pltpu.make_async_remote_copy(
                src_ref=ref.at[pl.ds(sx, wx), pl.ds(sy, wy), :],
                dst_ref=ref.at[pl.ds(tx_, wx), pl.ds(ty_, wy), :],
                send_sem=halo_send.at[slot, index],
                recv_sem=halo_recv.at[slot, index],
                device_id=(to_g, to_b),
                device_id_type=pl.DeviceIdType.MESH,
            )
            yield sends, receives, copy

    def halo_start(*args):
        for sends, _, copy in halo_copies(*args):
            pl.when(sends)(copy.start)

    def halo_wait(*args):
        for _, receives, copy in halo_copies(*args):
            pl.when(receives)(copy.wait_recv)

    def halo_sent(*args):
        for sends, _, copy in halo_copies(*args):
            pl.when(sends)(copy.wait_send)

    def gather_start(which):
        mine = slots[which].at[me]

        def body(go, bo):
            pltpu.make_async_remote_copy(
                src_ref=mine,
                dst_ref=mine,
                send_sem=all_send.at[which],
                recv_sem=all_recv.at[which],
                device_id=(go, bo),
                device_id_type=pl.DeviceIdType.MESH,
            ).start()

        others(body)

    def gather_wait(which, sem):
        part = slots[which].at[pl.ds(0, count - 1)]
        pltpu.make_async_copy(part, part, sem.at[which]).wait()

    def fill(x, _):
        for y in tiles(0, ny):
            tag = tags[x, pl.ds(y, 8), :]
            value = jnp.full(tag.shape, coef[0], jnp.float32)
            for region in range(1, coef.shape[0]):
                value = jnp.where(tag == region, coef[region], value)
            L[0].C[HX + x, pl.ds(YO + y, 8), :] = value * rough[x, pl.ds(y, 8), :] * 0.5
            f0[HX + x, pl.ds(YO + y, 8), :] = source[x, pl.ds(y, 8), :]

    each_x(0, nx, 1, fill)
    coef_pairs(L[0], R0)
    coarse_rows(L[0], R0, 0.125, L[1].C, HX, YO)
    coef_pairs(L[1], R1)
    coarse_rows(L[1], R1, 0.125, L[2].C, HX, YO)
    coef_pairs(L[2], R2)
    slots[0][me] = packed(L[2], R2, 0.125)

    pl.semaphore_wait(barrier, count - 1)
    start = [(L[0].C, L[0], 7, 0), (f0, L[0], 6, 1), (L[1].C, L[1], 7, 2), (L[2].C, L[2], 7, 3)]
    for args in start:
        halo_start(*args)
    gather_start(0)
    halo_wait(*start[0])
    operators(L[0], 6)
    halo_wait(*start[1])
    first_sweep(L[0], f0, L[0].VA, 6)
    sweep(L[0], f0, L[0].VA, L[0].VB, 5)
    sent = list(start)

    for cycle in range(2):
        wide = 6 if cycle == 0 else 4
        if cycle == 1:
            sweep(L[0], f0, L[0].VB, L[0].VA, 2)
            sweep(L[0], f0, L[0].VA, L[0].VB, 1)
        residual_pairs(L[0], f0, L[0].VB, R0)
        coarse_rows(L[0], R0, 0.5, f1[cycle], HX, YO)
        args = (f1[cycle], L[1], 6, 4 + cycle)
        halo_start(*args)
        sent.append(args)
        if cycle == 1:
            def keep(x, _):
                at = (x, pl.ds(YO, ny), slice(None))
                kept[at] = L[0].VB[at]

            each_x(HX, nx, 1, keep)
            kept_args = (kept, L[0], 3, 8)
            halo_start(*kept_args)
            sent.append(kept_args)
        if cycle == 0:
            halo_wait(*start[2])
            operators(L[1], 6)
        halo_wait(*args)
        first_sweep(L[1], f1[cycle], L[1].VA, 6)
        sweep(L[1], f1[cycle], L[1].VA, L[1].VB, 5)
        residual_pairs(L[1], f1[cycle], L[1].VB, R1)
        coarse_rows(L[1], R1, 0.5, f2[cycle], HX, YO)
        args = (f2[cycle], L[2], 6, 6 + cycle)
        halo_start(*args)
        sent.append(args)
        if cycle == 0:
            halo_wait(*start[3])
            operators(L[2], 6)
        halo_wait(*args)
        first_sweep(L[2], f2[cycle], L[2].VA, 6)
        sweep(L[2], f2[cycle], L[2].VA, L[2].VB, 5)
        residual_pairs(L[2], f2[cycle], L[2].VB, R2)
        slots[1 + cycle][me] = packed(L[2], R2, 0.5)
        gather_start(1 + cycle)
        if cycle == 0:
            gather_wait(0, all_recv)
            unpack(slots[0], flat, L[3].C, ng, nb, tx, ty)
            operators(L[3], 0)
            coef_pairs(L[3], R3)
            coarse_rows(L[3], R3, 0.125, L[4].C, 2, GY)
            operators(L[4], 0)
        gather_wait(1 + cycle, all_recv)
        unpack(slots[1 + cycle], flat, f3, ng, nb, tx, ty)
        first_sweep(L[3], f3, L[3].VA, 0)
        sweep(L[3], f3, L[3].VA, L[3].VB, 0)
        residual_pairs(L[3], f3, L[3].VB, R3)
        coarse_rows(L[3], R3, 0.5, f4, 2, GY)
        krylov(L[4], f4, L[4].VB, L[4].VA)
        add_refined(L[3], L[3].VB, L[3].VB, L[4].VB, 2, GY, 0)
        sweep(L[3], f3, L[3].VB, L[3].VA, 0)
        sweep(L[3], f3, L[3].VA, L[3].VB, 0)
        add_refined(L[2], L[2].VB, L[2].VB, L[3].VB, GX + g * tx - wide // 2,
                    pl.multiple_of(GY - 4 + b * ty, 4), wide)
        sweep(L[2], f2[cycle], L[2].VB, L[2].VA, wide // 2 + 1)
        sweep(L[2], f2[cycle], L[2].VA, L[2].VB, wide // 2)
        add_refined(L[1], L[1].VB, L[1].VB, L[2].VB, HX - wide // 2, YO - 4, wide)
        sweep(L[1], f1[cycle], L[1].VB, L[1].VA, wide // 2 + 1)
        sweep(L[1], f1[cycle], L[1].VA, L[1].VB, wide // 2)
        if cycle == 1:
            halo_wait(*kept_args)
        before = L[0].VB if cycle == 0 else kept
        add_refined(L[0], before, L[0].VB, L[1].VB, HX - wide // 2, YO - 4, wide)
        sweep(L[0], f0, L[0].VB, L[0].VA, wide - 2)
        sweep(L[0], f0, L[0].VA, L[0].VB, wide - 3)

    def finish(x, i):
        for y in tiles(YO, YO + ny):
            at = (pl.ds(x, 2), pl.ds(y, 8), slice(None))
            to = (pl.ds(2 * i, 2), pl.ds(y - YO, 8), slice(None))
            center, total = off_diagonal(L[0], L[0].VB, x, 2, y, 8)
            out_v[to] = center
            out_r[to] = f0[at] - L[0].D[at] * center + total

    each_x(HX, nx, 2, finish)
    for args in sent:
        halo_sent(*args)
    for which in range(3):
        gather_wait(which, all_send)


def body(ng, nb, source_field, region_tags, region_coef, roughness):
    nx, ny, nz = source_field.shape
    f32 = jnp.float32
    shapes = []
    padded = [(((nx >> l) + 2 * HX, (ny >> l) + 2 * YO, nz)) for l in range(3)]
    tx, ty = nx >> 3, ny >> 3
    padded.append((ng * tx + 2 * GX, nb * ty + 2 * GY, nz))
    padded.append((ng * tx // 2 + 4, nb * ty // 2 + 2 * GY, nz))
    for shape in padded:
        shapes += [shape] * 7
    shapes += [padded[0], padded[1], padded[1], padded[2], padded[2], padded[3], padded[4], padded[0]]
    shapes += [(nx >> (l + 1), ny >> l, nz) for l in range(3)]
    shapes += [(ng * tx // 2, nb * ty, nz), (nb * ty, nz)]
    shapes += [(ng * nb, ty, nz)] * 3
    dma = pltpu.SemaphoreType.DMA
    vmem = pl.BlockSpec(memory_space=pltpu.VMEM)
    return pl.pallas_call(
        functools.partial(kernel, ng, nb),
        out_shape=[jax.ShapeDtypeStruct(source_field.shape, f32)] * 2,
        in_specs=[vmem, vmem, pl.BlockSpec(memory_space=pltpu.SMEM), vmem],
        out_specs=[vmem, vmem],
        scratch_shapes=[pltpu.VMEM(shape, f32) for shape in shapes]
        + [dma((9, 8)), dma((9, 8)), dma((3,)), dma((3,))],
        compiler_params=pltpu.CompilerParams(
            collective_id=0, has_side_effects=True, vmem_limit_bytes=60 * 1024 * 1024
        ),
    )(source_field, region_tags, region_coef, roughness)


def solution(mesh):
    spec = P("grp", "box", None)
    return jax.shard_map(
        functools.partial(body, mesh.shape["grp"], mesh.shape["box"]),
        mesh=mesh,
        in_specs=(spec, spec, P(), spec),
        out_specs=(spec, spec),
        check_vma=False,
    )
```

```python
import functools
import jax
import jax.numpy as jnp
from jax import lax
from jax.experimental import pallas as pl
from jax.experimental.pallas import tpu as pltpu
from jax.sharding import PartitionSpec as P

NB = 4
LANES = 128
HX = 8
YO = 16
GX = 4
GY = 8
DIRECTIONS = [(dx, dy) for dx in (-1, 0, 1) for dy in (-1, 0, 1) if (dx, dy) != (0, 0)]


class Level:
    def __init__(self, shift, nx, ny, x0, y0, ylo, yhi, step, zero, refs):
        self.shift, self.nx, self.ny, self.x0, self.y0 = shift, nx, ny, x0, y0
        self.ylo, self.yhi, self.step, self.zero = ylo, yhi, step, zero
        self.WX, self.WY, self.WZ, self.G, self.D, self.VA, self.VB = refs[:7]
        self.C = refs[7] if len(refs) > 7 else self.VA


def lane_index(shape):
    return lax.broadcasted_iota(jnp.int32, shape, len(shape) - 1)


def roll(values, shift):
    return pltpu.roll(values, shift % LANES, values.ndim - 1)


def pair_sum(values, shift):
    even = (lane_index(values.shape) // shift) % 2 == 0
    return values + jnp.where(even, roll(values, LANES - shift), roll(values, shift))


def off_diagonal(L, V, x, n, y, rows):
    down, up = y - 1 + L.zero, y + 1 + L.zero
    block = V[pl.ds(x - 1, n + 2), pl.ds(y, rows), :]
    center = block[1:-1]
    wx = L.WX[pl.ds(x, n + 1), pl.ds(y, rows), :]
    wz = L.WZ[pl.ds(x, n), pl.ds(y, rows), :]
    total = wz * roll(center, L.shift) + roll(wz * center, LANES - L.shift)
    total = total + (wx[:-1] * block[:-2] + wx[1:] * block[2:])
    total = total + (
        L.WY[pl.ds(x, n), pl.ds(y, rows), :] * V[pl.ds(x, n), pl.ds(down, rows), :]
        + L.WY[pl.ds(x, n), pl.ds(up, rows), :] * V[pl.ds(x, n), pl.ds(up, rows), :]
    )
    return center, total


def each_x(start, count, step, body):
    def run(i, carry):
        body(start + i * step, i)
        return carry

    lax.fori_loop(0, count // step, run, 0)


def tiles(lo, hi):
    return range(lo, hi, 8)


def store_all(stores):
    for ref, at, value in stores:
        ref[at] = value


def halo_range(L, k):
    count = -(-(L.nx + 2 * k) // L.step) * L.step
    return L.x0 - (count - L.nx) // 2, count


def operators(L, k):
    n = L.step

    def body(x, i):
        stores = []
        for y in tiles(L.ylo, L.yhi):
            at = (pl.ds(x, n), pl.ds(y, 8), slice(None))
            coef = L.C[pl.ds(x - 1, n + 2), pl.ds(y, 8), :]
            c = coef[1:-1]
            lane = lane_index(c.shape)
            low = jnp.where(lane < L.shift, 0.0, roll(c, L.shift))
            high = jnp.where(lane >= LANES - L.shift, 0.0, roll(c, LANES - L.shift))
            before = L.C[pl.ds(x, n), pl.ds(y - 1 + L.zero, 8), :]
            after = L.C[pl.ds(x, n), pl.ds(y + 1 + L.zero, 8), :]
            diag = 6.0 * c + (coef[:-2] + coef[2:]) + (low + high) + (before + after)
            inside = c > 0.0
            stores += [
                (L.WX, (pl.ds(x, n + 1), pl.ds(y, 8), slice(None)), coef[1:] + coef[:-1]),
                (L.WY, at, c + before),
                (L.WZ, at, jnp.where(lane < L.shift, 0.0, c + low)),
                (L.G, at, jnp.where(inside, 0.8 / jnp.where(inside, diag, 1.0), 0.0)),
            ]
            if L.y0 <= y < L.y0 + L.ny:
                stores.append((L.D, (pl.ds(x, n), pl.ds(y - L.y0, 8), slice(None)), diag))
            if y + 8 == L.yhi:
                last = (pl.ds(x, n), pl.ds(L.yhi, 8), slice(None))
                stores.append((L.WY, last, L.C[last] + L.C[pl.ds(x, n), pl.ds(L.yhi - 1 + L.zero, 8), :]))
        store_all(stores)

    start, count = halo_range(L, k)
    each_x(start, count, n, body)


def first_sweep(L, F, dst, k):
    def body(x, i):
        stores = []
        for y in tiles(L.ylo, L.yhi):
            at = (pl.ds(x, L.step), pl.ds(y, 8), slice(None))
            stores.append((dst, at, L.G[at] * F[at]))
        store_all(stores)

    start, count = halo_range(L, k)
    each_x(start, count, L.step, body)


def sweep(L, F, src, dst, k):
    def body(x, i):
        stores = []
        for y in tiles(L.ylo, L.yhi):
            at = (pl.ds(x, L.step), pl.ds(y, 8), slice(None))
            center, total = off_diagonal(L, src, x, L.step, y, 8)
            stores.append((dst, at, 0.2 * center + L.G[at] * (F[at] + total)))
        store_all(stores)

    start, count = halo_range(L, k)
    each_x(start, count, L.step, body)


def residual_pairs(L, F, V, R):
    n = L.step

    def body(x, i):
        stores = []
        for y in tiles(L.y0, L.y0 + L.ny):
            at = (pl.ds(x, n), pl.ds(y, 8), slice(None))
            center, total = off_diagonal(L, V, x, n, y, 8)
            diag = L.D[pl.ds(x, n), pl.ds(y - L.y0, 8), :]
            left = F[at] - diag * center + total
            for p in range(n // 2):
                stores.append((R, (i * (n // 2) + p, pl.ds(y - L.y0, 8), slice(None)),
                               left[2 * p] + left[2 * p + 1]))
        store_all(stores)

    each_x(L.x0, L.nx, n, body)


def coef_pairs(L, R):
    n = L.step

    def body(x, i):
        for y in tiles(L.y0, L.y0 + L.ny):
            c = L.C[pl.ds(x, n), pl.ds(y, 8), :]
            for p in range(n // 2):
                R[i * (n // 2) + p, pl.ds(y - L.y0, 8), :] = c[2 * p] + c[2 * p + 1]

    each_x(L.x0, L.nx, n, body)


def coarse_row(L, R, i, factor):
    half = L.ny // 2
    rows = R[i, pl.ds(0, half, stride=2), :] + R[i, pl.ds(1, half, stride=2), :]
    return pair_sum(rows, L.shift) * factor


def coarse_rows(L, R, factor, dst, x0, y0):
    count = L.nx // 2
    n = 8 if count % 8 == 0 else 4

    def body(i, _):
        rows = [coarse_row(L, R, i + p, factor) for p in range(n)]
        for p in range(n):
            dst[x0 + i + p, pl.ds(y0, L.ny // 2), :] = rows[p]

    each_x(0, count, n, body)


def packed(L, R, factor):
    count = L.nx // 2
    rows = [coarse_row(L, R, i, factor) for i in range(count)]
    which = lane_index(rows[0].shape) % count
    out = rows[0]
    for i in range(1, count):
        out = jnp.where(which == i, rows[i], out)
    return out


def unpack(slots, flat, dst, ng, nb, tx, ty):
    def gather(g, _):
        for b in range(nb):
            flat[g, pl.ds(b * ty, ty), :] = slots[g * nb + b]

    def body(g, _):
        for y in tiles(0, nb * ty):
            rows = flat[g, pl.ds(y, 8), :]
            rolled = {d: roll(rows, d) for d in range(1 - tx, tx)}
            which = lane_index(rows.shape) % tx
            for i in range(tx):
                out = rolled[-i]
                for d in range(1, tx):
                    out = jnp.where(which == d, rolled[d - i], out)
                dst[GX + g * tx + i, pl.ds(GY + y, 8), :] = out

    each_x(0, ng, 1, gather)
    each_x(0, ng, 1, body)


def add_refined(L, src, dst, E, ex, ey, k):
    half = (L.yhi - L.ylo) // 2

    def body(x, i):
        stores = []
        for p in range(2):
            e = E[ex + 2 * i + p, pl.ds(ey, half), :]
            for dx in range(2):
                for phase in range(2):
                    at = (x + 2 * p + dx, pl.ds(L.ylo + phase, half, stride=2), slice(None))
                    stores.append((dst, at, src[at] + e))
        store_all(stores)

    each_x(L.x0 - k, L.nx + 2 * k, 4, body)


def total_of(values):
    return jnp.sum(values, axis=(0, 1, 2), keepdims=True)


def krylov(L, F, E, V):
    at = (pl.ds(L.x0, L.nx), pl.ds(L.y0, L.ny), slice(None))
    remain = F[at]
    direction = remain
    values = jnp.zeros_like(remain)
    norm_now = total_of(remain * remain)
    for step in range(NB):
        V[at] = direction
        _, total = off_diagonal(L, V, L.x0, L.nx, L.y0, L.ny)
        image = L.D[pl.ds(L.x0, L.nx)] * direction - total
        alpha = norm_now / total_of(direction * image)
        values = values + alpha * direction
        if step < NB - 1:
            remain = remain - alpha * image
            norm_next = total_of(remain * remain)
            direction = remain + (norm_next / norm_now) * direction
            norm_now = norm_next
    E[at] = values


def zero(ref):
    def body(i, _):
        ref[i] = jnp.zeros(ref.shape[1:], ref.dtype)

    each_x(0, ref.shape[0], 1, body)


def zero_halo(ref, L, k):
    y0, y1, nx = L.y0, L.y0 + L.ny, L.nx

    def ends(i, _):
        rows = jnp.zeros((y1 - y0 + 16, LANES), ref.dtype)
        ref[HX - k + i, pl.ds(y0 - 8, y1 - y0 + 16), :] = rows
        ref[HX + nx + i, pl.ds(y0 - 8, y1 - y0 + 16), :] = rows

    def sides(x, _):
        ref[x, pl.ds(y0 - 8, 8), :] = jnp.zeros((8, LANES), ref.dtype)
        ref[x, pl.ds(y1, 8), :] = jnp.zeros((8, LANES), ref.dtype)

    each_x(0, k, 1, ends)
    each_x(HX, nx, 1, sides)


def kernel(ng, nb, source, tags, coef, rough, out_v, out_r, *scratch):
    scratch = list(scratch)

    def take(count):
        taken = scratch[:count]
        del scratch[:count]
        return taken

    g, b = lax.axis_index("grp"), lax.axis_index("box")
    me = g * nb + b
    count = ng * nb
    none = lax.div(g, jnp.int32(ng))

    nx, ny = source.shape[0], source.shape[1]
    L = []
    for l in range(3):
        L.append(Level(1 << l, nx >> l, ny >> l, HX, YO, 8, (ny >> l) + 24, 4, none, take(8)))
    tx, ty = nx >> 3, ny >> 3
    L.append(Level(8, ng * tx, nb * ty, GX, GY, GY, GY + nb * ty, 4 if nb * ty <= 32 else 2, none, take(7)))
    L.append(Level(16, ng * tx // 2, nb * ty // 2, 2, GY, GY, GY + nb * ty // 2, ng * tx // 2, none, take(7)))
    f0, f1a, f1b, f2a, f2b, f3, f4, kept = take(8)
    f1, f2 = (f1a, f1b), (f2a, f2b)
    R0, R3 = take(2)
    R1 = R2 = R0
    flat = R3
    slots = take(3)
    halo_send, halo_recv, all_send, all_recv = take(4)

    for ref, level in [(L[0].C, L[0]), (f0, L[0]), (kept, L[0]), (L[1].C, L[1]), (f1a, L[1]),
                       (f1b, L[1]), (L[2].C, L[2]), (f2a, L[2]), (f2b, L[2])]:
        zero_halo(ref, level, 7)

    barrier = pltpu.get_barrier_semaphore()

    def others(body):
        def run(i, carry):
            other = lax.rem(me + i, count)
            body(other // nb, lax.rem(other, nb))
            return carry

        lax.fori_loop(1, count, run, 0)

    others(lambda go, bo: pl.semaphore_signal(
        barrier, inc=1, device_id=(go, bo), device_id_type=pl.DeviceIdType.MESH))

    def halo_copies(ref, level, h, slot, src=None):
        for index, (dx, dy) in enumerate(DIRECTIONS):
            n, m = level.nx, level.ny
            sx, tx_, wx = {-1: (HX, HX + n, h), 0: (HX, HX, n), 1: (HX + n - h, HX - h, h)}[dx]
            sy, ty_, wy = {-1: (YO, YO + m, 8), 0: (YO, YO, m), 1: (YO + m - 8, YO - 8, 8)}[dy]
            to_g, to_b, from_g, from_b = g + dx, b + dy, g - dx, b - dy
            sends = (to_g >= 0) & (to_g < ng) & (to_b >= 0) & (to_b < nb)
            receives = (from_g >= 0) & (from_g < ng) & (from_b >= 0) & (from_b < nb)
            lead, side = (0, 0) if src is None else (HX, YO)
            copy = pltpu.make_async_remote_copy(
                src_ref=(ref if src is None else src).at[pl.ds(sx - lead, wx), pl.ds(sy - side, wy), :],
                dst_ref=ref.at[pl.ds(tx_, wx), pl.ds(ty_, wy), :],
                send_sem=halo_send.at[slot, index],
                recv_sem=halo_recv.at[slot, index],
                device_id=(to_g, to_b),
                device_id_type=pl.DeviceIdType.MESH,
            )
            yield sends, receives, copy

    def halo_start(*args):
        for sends, _, copy in halo_copies(*args):
            pl.when(sends)(copy.start)

    def halo_wait(*args):
        for _, receives, copy in halo_copies(*args):
            pl.when(receives)(copy.wait_recv)

    def halo_sent(*args):
        for sends, _, copy in halo_copies(*args):
            pl.when(sends)(copy.wait_send)

    def gather_start(which):
        mine = slots[which].at[me]

        def body(go, bo):
            pltpu.make_async_remote_copy(
                src_ref=mine,
                dst_ref=mine,
                send_sem=all_send.at[which],
                recv_sem=all_recv.at[which],
                device_id=(go, bo),
                device_id_type=pl.DeviceIdType.MESH,
            ).start()

        others(body)

    def gather_wait(which, sem):
        part = slots[which].at[pl.ds(0, count - 1)]
        pltpu.make_async_copy(part, part, sem.at[which]).wait()

    def fill(x, _):
        stores = []
        for dx in range(2):
            for y in tiles(0, ny):
                tag = tags[x + dx, pl.ds(y, 8), :]
                value = jnp.full(tag.shape, coef[0], jnp.float32)
                for region in range(1, coef.shape[0]):
                    value = jnp.where(tag == region, coef[region], value)
                at = (HX + x + dx, pl.ds(YO + y, 8), slice(None))
                stores.append((L[0].C, at, value * rough[x + dx, pl.ds(y, 8), :] * 0.5))
                stores.append((f0, at, source[x + dx, pl.ds(y, 8), :]))
        store_all(stores)

    each_x(0, nx, 2, fill)
    pl.semaphore_wait(barrier, count - 1)
    start = [(L[0].C, L[0], 7, 0), (f0, L[0], 6, 1, source), (L[1].C, L[1], 7, 2), (L[2].C, L[2], 7, 3)]
    halo_start(*start[0])
    halo_start(*start[1])
    for level in L[3:]:
        zero(level.VA)
        zero(level.VB)
    coef_pairs(L[0], R0)
    coarse_rows(L[0], R0, 0.125, L[1].C, HX, YO)
    coef_pairs(L[1], R1)
    coarse_rows(L[1], R1, 0.125, L[2].C, HX, YO)
    coef_pairs(L[2], R2)
    slots[0][me] = packed(L[2], R2, 0.125)
    halo_start(*start[2])
    halo_start(*start[3])
    gather_start(0)
    halo_wait(*start[0])
    operators(L[0], 6)
    halo_wait(*start[1])
    first_sweep(L[0], f0, L[0].VA, 6)
    sweep(L[0], f0, L[0].VA, L[0].VB, 5)
    sent = list(start)

    for cycle in range(2):
        wide = 6 if cycle == 0 else 4
        if cycle == 1:
            sweep(L[0], f0, L[0].VB, L[0].VA, 2)
            sweep(L[0], f0, L[0].VA, L[0].VB, 1)
        residual_pairs(L[0], f0, L[0].VB, R0)
        coarse_rows(L[0], R0, 0.5, f1[cycle], HX, YO)
        args = (f1[cycle], L[1], 6, 4 + cycle)
        halo_start(*args)
        sent.append(args)
        if cycle == 1:
            def keep(x, _):
                at = (x, pl.ds(YO, ny), slice(None))
                kept[at] = L[0].VB[at]

            each_x(HX, nx, 1, keep)
            kept_args = (kept, L[0], 3, 8)
            halo_start(*kept_args)
            sent.append(kept_args)
        if cycle == 0:
            halo_wait(*start[2])
            operators(L[1], 6)
        halo_wait(*args)
        first_sweep(L[1], f1[cycle], L[1].VA, 6)
        sweep(L[1], f1[cycle], L[1].VA, L[1].VB, 5)
        residual_pairs(L[1], f1[cycle], L[1].VB, R1)
        coarse_rows(L[1], R1, 0.5, f2[cycle], HX, YO)
        args = (f2[cycle], L[2], 6, 6 + cycle)
        halo_start(*args)
        sent.append(args)
        if cycle == 0:
            halo_wait(*start[3])
            operators(L[2], 6)
        halo_wait(*args)
        first_sweep(L[2], f2[cycle], L[2].VA, 6)
        sweep(L[2], f2[cycle], L[2].VA, L[2].VB, 5)
        residual_pairs(L[2], f2[cycle], L[2].VB, R2)
        slots[1 + cycle][me] = packed(L[2], R2, 0.5)
        gather_start(1 + cycle)
        if cycle == 0:
            gather_wait(0, all_recv)
            unpack(slots[0], flat, L[3].C, ng, nb, tx, ty)
            operators(L[3], 0)
            coef_pairs(L[3], R3)
            coarse_rows(L[3], R3, 0.125, L[4].C, 2, GY)
            operators(L[4], 0)
        gather_wait(1 + cycle, all_recv)
        unpack(slots[1 + cycle], flat, f3, ng, nb, tx, ty)
        first_sweep(L[3], f3, L[3].VA, 0)
        sweep(L[3], f3, L[3].VA, L[3].VB, 0)
        residual_pairs(L[3], f3, L[3].VB, R3)
        coarse_rows(L[3], R3, 0.5, f4, 2, GY)
        krylov(L[4], f4, L[4].VB, L[4].VA)
        add_refined(L[3], L[3].VB, L[3].VB, L[4].VB, 2, GY, 0)
        sweep(L[3], f3, L[3].VB, L[3].VA, 0)
        sweep(L[3], f3, L[3].VA, L[3].VB, 0)
        add_refined(L[2], L[2].VB, L[2].VB, L[3].VB, GX + g * tx - wide // 2,
                    pl.multiple_of(GY - 4 + b * ty, 4), wide)
        sweep(L[2], f2[cycle], L[2].VB, L[2].VA, wide // 2 + 1)
        sweep(L[2], f2[cycle], L[2].VA, L[2].VB, wide // 2)
        add_refined(L[1], L[1].VB, L[1].VB, L[2].VB, HX - wide // 2, YO - 4, wide)
        sweep(L[1], f1[cycle], L[1].VB, L[1].VA, wide // 2 + 1)
        sweep(L[1], f1[cycle], L[1].VA, L[1].VB, wide // 2)
        if cycle == 1:
            halo_wait(*kept_args)
        before = L[0].VB if cycle == 0 else kept
        add_refined(L[0], before, L[0].VB, L[1].VB, HX - wide // 2, YO - 4, wide)
        sweep(L[0], f0, L[0].VB, L[0].VA, wide - 2)
        sweep(L[0], f0, L[0].VA, L[0].VB, wide - 3)

    def finish(x, i):
        for y in tiles(YO, YO + ny):
            at = (pl.ds(x, 2), pl.ds(y, 8), slice(None))
            to = (pl.ds(2 * i, 2), pl.ds(y - YO, 8), slice(None))
            center, total = off_diagonal(L[0], L[0].VB, x, 2, y, 8)
            out_v[to] = center
            out_r[to] = f0[at] - L[0].D[pl.ds(x, 2), pl.ds(y - YO, 8), :] * center + total

    each_x(HX, nx, 2, finish)
    for args in sent:
        halo_sent(*args)
    for which in range(3):
        gather_wait(which, all_send)


def body(ng, nb, source_field, region_tags, region_coef, roughness):
    nx, ny, nz = source_field.shape
    f32 = jnp.float32
    shapes = []
    padded = [(((nx >> l) + 2 * HX, (ny >> l) + 2 * YO, nz)) for l in range(3)]
    tx, ty = nx >> 3, ny >> 3
    padded.append((ng * tx + 2 * GX, nb * ty + 2 * GY, nz))
    padded.append((ng * tx // 2 + 4, nb * ty // 2 + 2 * GY, nz))
    for index, shape in enumerate(padded):
        own = (shape[0], shape[1] - 2 * (YO if index < 3 else GY), nz)
        shapes += [shape] * 4 + [own] + [shape] * (3 if index < 3 else 2)
    shapes += [padded[0], padded[1], padded[1], padded[2], padded[2], padded[3], padded[4], padded[0]]
    shapes += [(nx // 2, ny, nz), (ng * tx // 2, nb * ty, nz)]
    shapes += [(ng * nb, ty, nz)] * 3
    dma = pltpu.SemaphoreType.DMA
    vmem = pl.BlockSpec(memory_space=pltpu.VMEM)
    return pl.pallas_call(
        functools.partial(kernel, ng, nb),
        out_shape=[jax.ShapeDtypeStruct(source_field.shape, f32)] * 2,
        in_specs=[vmem, vmem, pl.BlockSpec(memory_space=pltpu.SMEM), vmem],
        out_specs=[vmem, vmem],
        scratch_shapes=[pltpu.VMEM(shape, f32) for shape in shapes]
        + [dma((9, 8)), dma((9, 8)), dma((3,)), dma((3,))],
        compiler_params=pltpu.CompilerParams(
            collective_id=0, has_side_effects=True, vmem_limit_bytes=63 * 1024 * 1024
        ),
    )(source_field, region_tags, region_coef, roughness)


def solution(mesh):
    spec = P("grp", "box", None)
    return jax.shard_map(
        functools.partial(body, mesh.shape["grp"], mesh.shape["box"]),
        mesh=mesh,
        in_specs=(spec, spec, P(), spec),
        out_specs=(spec, spec),
        check_vma=False,
    )
```

```python
import functools
import jax
import jax.numpy as jnp
from jax import lax
from jax.experimental import pallas as pl
from jax.experimental.pallas import tpu as pltpu
from jax.sharding import PartitionSpec as P

NB = 4
LANES = 128
HX = 8
YO = 16
GX = 4
GY = 8
DIRECTIONS = [(dx, dy) for dx in (-1, 0, 1) for dy in (-1, 0, 1) if (dx, dy) != (0, 0)]


class Level:
    def __init__(self, shift, nx, ny, x0, y0, ylo, yhi, step, zero, refs):
        self.shift, self.nx, self.ny, self.x0, self.y0 = shift, nx, ny, x0, y0
        self.ylo, self.yhi, self.step, self.zero = ylo, yhi, step, zero
        self.WX, self.WY, self.WZ, self.G, self.D, self.VA, self.VB = refs[:7]
        self.C = refs[7] if len(refs) > 7 else self.VA


def lane_index(shape):
    return lax.broadcasted_iota(jnp.int32, shape, len(shape) - 1)


def roll(values, shift):
    return pltpu.roll(values, shift % LANES, values.ndim - 1)


def pair_sum(values, shift):
    even = (lane_index(values.shape) & shift) == 0
    return values + jnp.where(even, roll(values, LANES - shift), roll(values, shift))


def off_diagonal(L, V, x, n, y, rows):
    down, up = y - 1 + L.zero, y + 1 + L.zero
    block = V[pl.ds(x - 1, n + 2), pl.ds(y, rows), :]
    center = block[1:-1]
    wx = L.WX[pl.ds(x, n + 1), pl.ds(y, rows), :]
    wz = L.WZ[pl.ds(x, n), pl.ds(y, rows), :]
    total = wz * roll(center, L.shift) + roll(wz * center, LANES - L.shift)
    total = total + (wx[:-1] * block[:-2] + wx[1:] * block[2:])
    total = total + (
        L.WY[pl.ds(x, n), pl.ds(y, rows), :] * V[pl.ds(x, n), pl.ds(down, rows), :]
        + L.WY[pl.ds(x, n), pl.ds(up, rows), :] * V[pl.ds(x, n), pl.ds(up, rows), :]
    )
    return center, total


def each_x(start, count, step, body):
    def run(i, carry):
        body(start + i * step, i)
        return carry

    lax.fori_loop(0, count // step, run, 0)


def tiles(lo, hi):
    return range(lo, hi, 8)


def store_all(stores):
    for ref, at, value in stores:
        ref[at] = value


def halo_range(L, k):
    count = -(-(L.nx + 2 * k) // L.step) * L.step
    return L.x0 - (count - L.nx) // 2, count


def operators(L, k):
    n = L.step

    def body(x, i):
        stores = []
        for y in tiles(L.ylo, L.yhi):
            at = (pl.ds(x, n), pl.ds(y, 8), slice(None))
            coef = L.C[pl.ds(x - 1, n + 2), pl.ds(y, 8), :]
            c = coef[1:-1]
            lane = lane_index(c.shape)
            low = jnp.where(lane < L.shift, 0.0, roll(c, L.shift))
            high = jnp.where(lane >= LANES - L.shift, 0.0, roll(c, LANES - L.shift))
            before = L.C[pl.ds(x, n), pl.ds(y - 1 + L.zero, 8), :]
            after = L.C[pl.ds(x, n), pl.ds(y + 1 + L.zero, 8), :]
            diag = 6.0 * c + (coef[:-2] + coef[2:]) + (low + high) + (before + after)
            inside = c > 0.0
            stores += [
                (L.WX, (pl.ds(x, n + 1), pl.ds(y, 8), slice(None)), coef[1:] + coef[:-1]),
                (L.WY, at, c + before),
                (L.WZ, at, jnp.where(lane < L.shift, 0.0, c + low)),
                (L.G, at, jnp.where(inside, 0.8 / jnp.where(inside, diag, 1.0), 0.0)),
            ]
            if L.y0 <= y < L.y0 + L.ny:
                stores.append((L.D, (pl.ds(x, n), pl.ds(y - L.y0, 8), slice(None)), diag))
            if y + 8 == L.yhi:
                last = (pl.ds(x, n), pl.ds(L.yhi, 8), slice(None))
                stores.append((L.WY, last, L.C[last] + L.C[pl.ds(x, n), pl.ds(L.yhi - 1 + L.zero, 8), :]))
        store_all(stores)

    start, count = halo_range(L, k)
    each_x(start, count, n, body)


def first_sweep(L, F, dst, k):
    def body(x, i):
        stores = []
        for y in tiles(L.ylo, L.yhi):
            at = (pl.ds(x, L.step), pl.ds(y, 8), slice(None))
            stores.append((dst, at, L.G[at] * F[at]))
        store_all(stores)

    start, count = halo_range(L, k)
    each_x(start, count, L.step, body)


def sweep(L, F, src, dst, k):
    def body(x, i):
        stores = []
        for y in tiles(L.ylo, L.yhi):
            at = (pl.ds(x, L.step), pl.ds(y, 8), slice(None))
            center, total = off_diagonal(L, src, x, L.step, y, 8)
            stores.append((dst, at, 0.2 * center + L.G[at] * (F[at] + total)))
        store_all(stores)

    start, count = halo_range(L, k)
    each_x(start, count, L.step, body)


def residual_pairs(L, F, V, R):
    n = L.step

    def body(x, i):
        stores = []
        for y in tiles(L.y0, L.y0 + L.ny):
            at = (pl.ds(x, n), pl.ds(y, 8), slice(None))
            center, total = off_diagonal(L, V, x, n, y, 8)
            diag = L.D[pl.ds(x, n), pl.ds(y - L.y0, 8), :]
            left = F[at] - diag * center + total
            for p in range(n // 2):
                stores.append((R, (i * (n // 2) + p, pl.ds(y - L.y0, 8), slice(None)),
                               left[2 * p] + left[2 * p + 1]))
        store_all(stores)

    each_x(L.x0, L.nx, n, body)


def coef_pairs(L, R):
    n = L.step

    def body(x, i):
        for y in tiles(L.y0, L.y0 + L.ny):
            c = L.C[pl.ds(x, n), pl.ds(y, 8), :]
            for p in range(n // 2):
                R[i * (n // 2) + p, pl.ds(y - L.y0, 8), :] = c[2 * p] + c[2 * p + 1]

    each_x(L.x0, L.nx, n, body)


def coarse_row(L, R, i, factor):
    half = L.ny // 2
    rows = R[i, pl.ds(0, half, stride=2), :] + R[i, pl.ds(1, half, stride=2), :]
    return pair_sum(rows, L.shift) * factor


def coarse_rows(L, R, factor, dst, x0, y0):
    count = L.nx // 2
    n = 8 if count % 8 == 0 else 4

    def body(i, _):
        rows = [coarse_row(L, R, i + p, factor) for p in range(n)]
        for p in range(n):
            dst[x0 + i + p, pl.ds(y0, L.ny // 2), :] = rows[p]

    each_x(0, count, n, body)


def packed(L, R, factor):
    count = L.nx // 2
    rows = [coarse_row(L, R, i, factor) for i in range(count)]
    which = lane_index(rows[0].shape) & (count - 1)
    out = rows[0]
    for i in range(1, count):
        out = jnp.where(which == i, rows[i], out)
    return out


def unpack(slots, flat, dst, ng, nb, tx, ty):
    def gather(g, _):
        for b in range(nb):
            flat[g, pl.ds(b * ty, ty), :] = slots[g * nb + b]

    def body(g, _):
        for y in tiles(0, nb * ty):
            rows = flat[g, pl.ds(y, 8), :]
            rolled = {d: roll(rows, d) for d in range(1 - tx, tx)}
            which = lane_index(rows.shape) & (tx - 1)
            for i in range(tx):
                out = rolled[-i]
                for d in range(1, tx):
                    out = jnp.where(which == d, rolled[d - i], out)
                dst[GX + g * tx + i, pl.ds(GY + y, 8), :] = out

    each_x(0, ng, 1, gather)
    each_x(0, ng, 1, body)


def add_refined(L, src, dst, E, ex, ey, k):
    half = (L.yhi - L.ylo) // 2

    def body(x, i):
        stores = []
        for p in range(2):
            e = E[ex + 2 * i + p, pl.ds(ey, half), :]
            for dx in range(2):
                for phase in range(2):
                    at = (x + 2 * p + dx, pl.ds(L.ylo + phase, half, stride=2), slice(None))
                    stores.append((dst, at, src[at] + e))
        store_all(stores)

    each_x(L.x0 - k, L.nx + 2 * k, 4, body)


def total_of(values):
    return jnp.sum(values, axis=(0, 1, 2), keepdims=True)


def krylov(L, F, E, V):
    at = (pl.ds(L.x0, L.nx), pl.ds(L.y0, L.ny), slice(None))
    remain = F[at]
    direction = remain
    values = jnp.zeros_like(remain)
    norm_now = total_of(remain * remain)
    for step in range(NB):
        V[at] = direction
        _, total = off_diagonal(L, V, L.x0, L.nx, L.y0, L.ny)
        image = L.D[pl.ds(L.x0, L.nx)] * direction - total
        alpha = norm_now / total_of(direction * image)
        values = values + alpha * direction
        if step < NB - 1:
            remain = remain - alpha * image
            norm_next = total_of(remain * remain)
            direction = remain + (norm_next / norm_now) * direction
            norm_now = norm_next
    E[at] = values


def zero(ref):
    def body(i, _):
        ref[i] = jnp.zeros(ref.shape[1:], ref.dtype)

    each_x(0, ref.shape[0], 1, body)


def zero_halo(ref, L, k, edges):
    y0, y1, nx = L.y0, L.y0 + L.ny, L.nx

    def ends(start):
        for i in range(k):
            ref[start + i, pl.ds(y0 - 8, L.ny + 16), :] = jnp.zeros((L.ny + 16, LANES), ref.dtype)

    def side(y):
        def rows(x, _):
            ref[pl.ds(x, 8), pl.ds(y, 8), :] = jnp.zeros((8, 8, LANES), ref.dtype)

        each_x(0, ref.shape[0], 8, rows)

    first_x, last_x, first_y, last_y = edges
    pl.when(first_x)(lambda: ends(HX - k))
    pl.when(last_x)(lambda: ends(HX + nx))
    pl.when(first_y)(lambda: side(y0 - 8))
    pl.when(last_y)(lambda: side(y1))


def kernel(ng, nb, source, tags, coef, rough, out_v, out_r, *scratch):
    scratch = list(scratch)

    def take(count):
        taken = scratch[:count]
        del scratch[:count]
        return taken

    g, b = lax.axis_index("grp"), lax.axis_index("box")
    me = g * nb + b
    count = ng * nb
    none = lax.div(g, jnp.int32(ng))

    nx, ny = source.shape[0], source.shape[1]
    L = []
    for l in range(3):
        L.append(Level(1 << l, nx >> l, ny >> l, HX, YO, 8, (ny >> l) + 24, 4, none, take(8)))
    tx, ty = nx >> 3, ny >> 3
    L.append(Level(8, ng * tx, nb * ty, GX, GY, GY, GY + nb * ty, 4 if nb * ty <= 32 else 2, none, take(7)))
    L.append(Level(16, ng * tx // 2, nb * ty // 2, 2, GY, GY, GY + nb * ty // 2, ng * tx // 2, none, take(7)))
    f0, f1a, f1b, f2a, f2b, f3, f4, kept = take(8)
    f1, f2 = (f1a, f1b), (f2a, f2b)
    R0, R3 = take(2)
    R1 = R2 = R0
    flat = R3
    slots = take(3)
    halo_send, halo_recv, all_send, all_recv = take(4)

    edges = (g == 0, g == ng - 1, b == 0, b == nb - 1)
    for ref, level in [(L[0].C, L[0]), (f0, L[0]), (L[1].C, L[1]), (L[2].C, L[2])]:
        zero_halo(ref, level, 7, edges)

    barrier = pltpu.get_barrier_semaphore()

    all_g = [g] + [lax.rem(g + i, ng) for i in range(1, ng)]
    all_b = [b] + [lax.rem(b + i, nb) for i in range(1, nb)]

    def others(body):
        for i in range(ng):
            for j in range(nb):
                if i or j:
                    body(all_g[i], all_b[j])

    others(lambda go, bo: pl.semaphore_signal(
        barrier, inc=1, device_id=(go, bo), device_id_type=pl.DeviceIdType.MESH))

    def halo_copies(ref, level, h, slot, src=None):
        for index, (dx, dy) in enumerate(DIRECTIONS):
            n, m = level.nx, level.ny
            sx, tx_, wx = {-1: (HX, HX + n, h), 0: (HX, HX, n), 1: (HX + n - h, HX - h, h)}[dx]
            sy, ty_, wy = {-1: (YO, YO + m, 8), 0: (YO, YO, m), 1: (YO + m - 8, YO - 8, 8)}[dy]
            to_g, to_b, from_g, from_b = g + dx, b + dy, g - dx, b - dy
            sends = (to_g >= 0) & (to_g < ng) & (to_b >= 0) & (to_b < nb)
            receives = (from_g >= 0) & (from_g < ng) & (from_b >= 0) & (from_b < nb)
            lead, side = (0, 0) if src is None else (HX, YO)
            copy = pltpu.make_async_remote_copy(
                src_ref=(ref if src is None else src).at[pl.ds(sx - lead, wx), pl.ds(sy - side, wy), :],
                dst_ref=ref.at[pl.ds(tx_, wx), pl.ds(ty_, wy), :],
                send_sem=halo_send.at[slot, index],
                recv_sem=halo_recv.at[slot, index],
                device_id=(to_g, to_b),
                device_id_type=pl.DeviceIdType.MESH,
            )
            yield sends, receives, copy

    def halo_start(*args):
        for sends, _, copy in halo_copies(*args):
            pl.when(sends)(copy.start)

    def halo_wait(*args):
        for _, receives, copy in halo_copies(*args):
            pl.when(receives)(copy.wait_recv)

    def halo_sent(*args):
        for sends, _, copy in halo_copies(*args):
            pl.when(sends)(copy.wait_send)

    def gather_start(which):
        mine = slots[which].at[me]

        def body(go, bo):
            pltpu.make_async_remote_copy(
                src_ref=mine,
                dst_ref=mine,
                send_sem=all_send.at[which],
                recv_sem=all_recv.at[which],
                device_id=(go, bo),
                device_id_type=pl.DeviceIdType.MESH,
            ).start()

        others(body)

    def gather_wait(which, sem):
        part = slots[which].at[pl.ds(0, count - 1)]
        pltpu.make_async_copy(part, part, sem.at[which]).wait()

    def fill(x, _):
        stores = []
        for dx in range(2):
            for y in tiles(0, ny):
                tag = tags[x + dx, pl.ds(y, 8), :]
                value = jnp.full(tag.shape, coef[0], jnp.float32)
                for region in range(1, coef.shape[0]):
                    value = jnp.where(tag == region, coef[region], value)
                at = (HX + x + dx, pl.ds(YO + y, 8), slice(None))
                stores.append((L[0].C, at, value * rough[x + dx, pl.ds(y, 8), :] * 0.5))
                stores.append((f0, at, source[x + dx, pl.ds(y, 8), :]))
        store_all(stores)

    for ref, level in [(f1a, L[1]), (f1b, L[1]), (f2a, L[2]), (f2b, L[2]), (kept, L[0])]:
        zero_halo(ref, level, 7, edges)
    each_x(0, nx, 2, fill)
    pl.semaphore_wait(barrier, count - 1)
    start = [(L[0].C, L[0], 7, 0), (f0, L[0], 6, 1, source), (L[1].C, L[1], 7, 2), (L[2].C, L[2], 7, 3)]
    halo_start(*start[0])
    halo_start(*start[1])
    for level in L[3:]:
        zero(level.VA)
        zero(level.VB)
    coef_pairs(L[0], R0)
    coarse_rows(L[0], R0, 0.125, L[1].C, HX, YO)
    coef_pairs(L[1], R1)
    coarse_rows(L[1], R1, 0.125, L[2].C, HX, YO)
    coef_pairs(L[2], R2)
    slots[0][me] = packed(L[2], R2, 0.125)
    halo_start(*start[2])
    halo_start(*start[3])
    gather_start(0)
    halo_wait(*start[0])
    operators(L[0], 6)
    halo_wait(*start[1])
    first_sweep(L[0], f0, L[0].VA, 6)
    sweep(L[0], f0, L[0].VA, L[0].VB, 5)
    sent = list(start)

    for cycle in range(2):
        wide = 6 if cycle == 0 else 4
        if cycle == 1:
            sweep(L[0], f0, L[0].VB, L[0].VA, 2)
            sweep(L[0], f0, L[0].VA, L[0].VB, 1)
        residual_pairs(L[0], f0, L[0].VB, R0)
        coarse_rows(L[0], R0, 0.5, f1[cycle], HX, YO)
        args = (f1[cycle], L[1], 6, 4 + cycle)
        halo_start(*args)
        sent.append(args)
        if cycle == 1:
            def keep(x, _):
                at = (x, pl.ds(YO, ny), slice(None))
                kept[at] = L[0].VB[at]

            each_x(HX, nx, 1, keep)
            kept_args = (kept, L[0], 3, 8)
            halo_start(*kept_args)
            sent.append(kept_args)
        if cycle == 0:
            halo_wait(*start[2])
            operators(L[1], 6)
        halo_wait(*args)
        first_sweep(L[1], f1[cycle], L[1].VA, 6)
        sweep(L[1], f1[cycle], L[1].VA, L[1].VB, 5)
        residual_pairs(L[1], f1[cycle], L[1].VB, R1)
        coarse_rows(L[1], R1, 0.5, f2[cycle], HX, YO)
        args = (f2[cycle], L[2], 6, 6 + cycle)
        halo_start(*args)
        sent.append(args)
        if cycle == 0:
            halo_wait(*start[3])
            operators(L[2], 6)
        halo_wait(*args)
        first_sweep(L[2], f2[cycle], L[2].VA, 6)
        sweep(L[2], f2[cycle], L[2].VA, L[2].VB, 5)
        residual_pairs(L[2], f2[cycle], L[2].VB, R2)
        slots[1 + cycle][me] = packed(L[2], R2, 0.5)
        gather_start(1 + cycle)
        if cycle == 0:
            gather_wait(0, all_recv)
            unpack(slots[0], flat, L[3].C, ng, nb, tx, ty)
            operators(L[3], 0)
            coef_pairs(L[3], R3)
            coarse_rows(L[3], R3, 0.125, L[4].C, 2, GY)
            operators(L[4], 0)
        gather_wait(1 + cycle, all_recv)
        unpack(slots[1 + cycle], flat, f3, ng, nb, tx, ty)
        first_sweep(L[3], f3, L[3].VA, 0)
        sweep(L[3], f3, L[3].VA, L[3].VB, 0)
        residual_pairs(L[3], f3, L[3].VB, R3)
        coarse_rows(L[3], R3, 0.5, f4, 2, GY)
        krylov(L[4], f4, L[4].VB, L[4].VA)
        add_refined(L[3], L[3].VB, L[3].VB, L[4].VB, 2, GY, 0)
        sweep(L[3], f3, L[3].VB, L[3].VA, 0)
        sweep(L[3], f3, L[3].VA, L[3].VB, 0)
        add_refined(L[2], L[2].VB, L[2].VB, L[3].VB, GX + g * tx - wide // 2,
                    pl.multiple_of(GY - 4 + b * ty, 4), wide)
        sweep(L[2], f2[cycle], L[2].VB, L[2].VA, wide // 2 + 1)
        sweep(L[2], f2[cycle], L[2].VA, L[2].VB, wide // 2)
        add_refined(L[1], L[1].VB, L[1].VB, L[2].VB, HX - wide // 2, YO - 4, wide)
        sweep(L[1], f1[cycle], L[1].VB, L[1].VA, wide // 2 + 1)
        sweep(L[1], f1[cycle], L[1].VA, L[1].VB, wide // 2)
        if cycle == 1:
            halo_wait(*kept_args)
        before = L[0].VB if cycle == 0 else kept
        add_refined(L[0], before, L[0].VB, L[1].VB, HX - wide // 2, YO - 4, wide)
        sweep(L[0], f0, L[0].VB, L[0].VA, wide - 2)
        sweep(L[0], f0, L[0].VA, L[0].VB, wide - 3)

    def finish(x, i):
        for y in tiles(YO, YO + ny):
            at = (pl.ds(x, 2), pl.ds(y, 8), slice(None))
            to = (pl.ds(2 * i, 2), pl.ds(y - YO, 8), slice(None))
            center, total = off_diagonal(L[0], L[0].VB, x, 2, y, 8)
            out_v[to] = center
            out_r[to] = f0[at] - L[0].D[pl.ds(x, 2), pl.ds(y - YO, 8), :] * center + total

    each_x(HX, nx, 2, finish)
    for args in sent:
        halo_sent(*args)
    for which in range(3):
        gather_wait(which, all_send)


def body(ng, nb, source_field, region_tags, region_coef, roughness):
    nx, ny, nz = source_field.shape
    f32 = jnp.float32
    shapes = []
    padded = [(((nx >> l) + 2 * HX, (ny >> l) + 2 * YO, nz)) for l in range(3)]
    tx, ty = nx >> 3, ny >> 3
    padded.append((ng * tx + 2 * GX, nb * ty + 2 * GY, nz))
    padded.append((ng * tx // 2 + 4, nb * ty // 2 + 2 * GY, nz))
    for index, shape in enumerate(padded):
        own = (shape[0], shape[1] - 2 * (YO if index < 3 else GY), nz)
        shapes += [shape] * 4 + [own] + [shape] * (3 if index < 3 else 2)
    shapes += [padded[0], padded[1], padded[1], padded[2], padded[2], padded[3], padded[4], padded[0]]
    shapes += [(nx // 2, ny, nz), (ng * tx // 2, nb * ty, nz)]
    shapes += [(ng * nb, ty, nz)] * 3
    dma = pltpu.SemaphoreType.DMA
    vmem = pl.BlockSpec(memory_space=pltpu.VMEM)
    return pl.pallas_call(
        functools.partial(kernel, ng, nb),
        out_shape=[jax.ShapeDtypeStruct(source_field.shape, f32)] * 2,
        in_specs=[vmem, vmem, pl.BlockSpec(memory_space=pltpu.SMEM), vmem],
        out_specs=[vmem, vmem],
        scratch_shapes=[pltpu.VMEM(shape, f32) for shape in shapes]
        + [dma((9, 8)), dma((9, 8)), dma((3,)), dma((3,))],
        compiler_params=pltpu.CompilerParams(
            collective_id=0, has_side_effects=True, vmem_limit_bytes=63 * 1024 * 1024
        ),
    )(source_field, region_tags, region_coef, roughness)


def solution(mesh):
    spec = P("grp", "box", None)
    return jax.shard_map(
        functools.partial(body, mesh.shape["grp"], mesh.shape["box"]),
        mesh=mesh,
        in_specs=(spec, spec, P(), spec),
        out_specs=(spec, spec),
        check_vma=False,
    )
```

```python
import functools
import jax
import jax.numpy as jnp
from jax import lax
from jax.experimental import pallas as pl
from jax.experimental.pallas import tpu as pltpu
from jax.sharding import PartitionSpec as P

NB = 4
LANES = 128
HX = 8
YO = 16
GX = 4
GY = 8
DIRECTIONS = [(dx, dy) for dx in (-1, 0, 1) for dy in (-1, 0, 1) if (dx, dy) != (0, 0)]


class Level:
    def __init__(self, shift, nx, ny, x0, y0, ylo, yhi, step, zero, refs):
        self.shift, self.nx, self.ny, self.x0, self.y0 = shift, nx, ny, x0, y0
        self.ylo, self.yhi, self.step, self.zero = ylo, yhi, step, zero
        self.WX, self.WY, self.WZ, self.G, self.D, self.VA, self.VB = refs[:7]
        self.C = refs[7] if len(refs) > 7 else self.VA


def lane_index(shape):
    return lax.broadcasted_iota(jnp.int32, shape, len(shape) - 1)


def roll(values, shift):
    return pltpu.roll(values, shift % LANES, values.ndim - 1)


def pair_sum(values, shift):
    even = (lane_index(values.shape) & shift) == 0
    return values + jnp.where(even, roll(values, LANES - shift), roll(values, shift))


def off_diagonal(L, V, x, n, y, rows):
    down, up = y - 1 + L.zero, y + 1 + L.zero
    block = V[pl.ds(x - 1, n + 2), pl.ds(y, rows), :]
    center = block[1:-1]
    wx = L.WX[pl.ds(x, n + 1), pl.ds(y, rows), :]
    wz = L.WZ[pl.ds(x, n), pl.ds(y, rows), :]
    total = wz * roll(center, L.shift) + roll(wz * center, LANES - L.shift)
    total = total + (wx[:-1] * block[:-2] + wx[1:] * block[2:])
    total = total + (
        L.WY[pl.ds(x, n), pl.ds(y, rows), :] * V[pl.ds(x, n), pl.ds(down, rows), :]
        + L.WY[pl.ds(x, n), pl.ds(up, rows), :] * V[pl.ds(x, n), pl.ds(up, rows), :]
    )
    return center, total


def each_x(start, count, step, body):
    def run(i, carry):
        body(start + i * step, i)
        return carry

    lax.fori_loop(0, count // step, run, 0)


def tiles(lo, hi):
    return range(lo, hi, 8)


def each_group(start, count, step, tiles_each, body):
    groups = count // step
    most = [u for u in range(1, groups + 1) if groups % u == 0 and u * tiles_each * step <= 128]
    unroll = groups if most[-1:] in ([], [1]) and groups < 12 else max(most + [1])

    def run(x, i):
        waiting = []
        for u in range(unroll):
            for ref, at, value in body(x + u * step, i * unroll + u):
                waiting.append((ref, at, value))
                while sum(v.size for _, _, v in waiting) > 20 * 1024:
                    store_all(waiting[:1])
                    del waiting[:1]
        store_all(waiting)

    each_x(start, count, step * unroll, run)


def store_all(stores):
    for ref, at, value in stores:
        ref[at] = value


def halo_range(L, k):
    count = -(-(L.nx + 2 * k) // L.step) * L.step
    return L.x0 - (count - L.nx) // 2, count


def operators(L, k):
    n = L.step

    def body(x, i):
        stores = []
        for y in tiles(L.ylo, L.yhi):
            at = (pl.ds(x, n), pl.ds(y, 8), slice(None))
            coef = L.C[pl.ds(x - 1, n + 2), pl.ds(y, 8), :]
            c = coef[1:-1]
            lane = lane_index(c.shape)
            low = jnp.where(lane < L.shift, 0.0, roll(c, L.shift))
            high = jnp.where(lane >= LANES - L.shift, 0.0, roll(c, LANES - L.shift))
            before = L.C[pl.ds(x, n), pl.ds(y - 1 + L.zero, 8), :]
            after = L.C[pl.ds(x, n), pl.ds(y + 1 + L.zero, 8), :]
            diag = 6.0 * c + (coef[:-2] + coef[2:]) + (low + high) + (before + after)
            inside = c > 0.0
            stores += [
                (L.WX, (pl.ds(x, n + 1), pl.ds(y, 8), slice(None)), coef[1:] + coef[:-1]),
                (L.WY, at, c + before),
                (L.WZ, at, jnp.where(lane < L.shift, 0.0, c + low)),
                (L.G, at, jnp.where(inside, 0.8 / jnp.where(inside, diag, 1.0), 0.0)),
            ]
            if L.y0 <= y < L.y0 + L.ny:
                stores.append((L.D, (pl.ds(x, n), pl.ds(y - L.y0, 8), slice(None)), diag))
            if y + 8 == L.yhi:
                last = (pl.ds(x, n), pl.ds(L.yhi, 8), slice(None))
                stores.append((L.WY, last, L.C[last] + L.C[pl.ds(x, n), pl.ds(L.yhi - 1 + L.zero, 8), :]))
        store_all(stores)

    start, count = halo_range(L, k)
    each_x(start, count, n, body)


def first_sweep(L, F, dst, k):
    def body(x, i):
        for y in tiles(L.ylo, L.yhi):
            at = (pl.ds(x, L.step), pl.ds(y, 8), slice(None))
            yield dst, at, L.G[at] * F[at]

    start, count = halo_range(L, k)
    each_group(start, count, L.step, (L.yhi - L.ylo) // 8, body)


def sweep(L, F, src, dst, k):
    def body(x, i):
        for y in tiles(L.ylo, L.yhi):
            at = (pl.ds(x, L.step), pl.ds(y, 8), slice(None))
            center, total = off_diagonal(L, src, x, L.step, y, 8)
            yield dst, at, 0.2 * center + L.G[at] * (F[at] + total)

    start, count = halo_range(L, k)
    each_group(start, count, L.step, (L.yhi - L.ylo) // 8, body)


def residual_pairs(L, F, V, R):
    n = L.step

    def body(x, i):
        for y in tiles(L.y0, L.y0 + L.ny):
            at = (pl.ds(x, n), pl.ds(y, 8), slice(None))
            center, total = off_diagonal(L, V, x, n, y, 8)
            diag = L.D[pl.ds(x, n), pl.ds(y - L.y0, 8), :]
            left = F[at] - diag * center + total
            for p in range(n // 2):
                at = (i * (n // 2) + p, pl.ds(y - L.y0, 8), slice(None))
                yield R, at, left[2 * p] + left[2 * p + 1]

    each_group(L.x0, L.nx, n, L.ny // 8, body)


def coef_pairs(L, R):
    n = L.step

    def body(x, i):
        for y in tiles(L.y0, L.y0 + L.ny):
            c = L.C[pl.ds(x, n), pl.ds(y, 8), :]
            for p in range(n // 2):
                R[i * (n // 2) + p, pl.ds(y - L.y0, 8), :] = c[2 * p] + c[2 * p + 1]

    each_x(L.x0, L.nx, n, body)


def coarse_row(L, R, i, factor):
    half = L.ny // 2
    rows = R[i, pl.ds(0, half, stride=2), :] + R[i, pl.ds(1, half, stride=2), :]
    return pair_sum(rows, L.shift) * factor


def coarse_rows(L, R, factor, dst, x0, y0):
    count = L.nx // 2
    n = 8 if count % 8 == 0 else 4

    def body(i, _):
        rows = [coarse_row(L, R, i + p, factor) for p in range(n)]
        for p in range(n):
            dst[x0 + i + p, pl.ds(y0, L.ny // 2), :] = rows[p]

    each_x(0, count, n, body)


def packed(L, R, factor):
    count = L.nx // 2
    rows = [coarse_row(L, R, i, factor) for i in range(count)]
    which = lane_index(rows[0].shape) & (count - 1)
    out = rows[0]
    for i in range(1, count):
        out = jnp.where(which == i, rows[i], out)
    return out


def unpack(slots, flat, dst, ng, nb, tx, ty):
    def gather(g, _):
        for b in range(nb):
            flat[g, pl.ds(b * ty, ty), :] = slots[g * nb + b]

    def body(g, _):
        for y in tiles(0, nb * ty):
            rows = flat[g, pl.ds(y, 8), :]
            rolled = {d: roll(rows, d) for d in range(1 - tx, tx)}
            which = lane_index(rows.shape) & (tx - 1)
            for i in range(tx):
                out = rolled[-i]
                for d in range(1, tx):
                    out = jnp.where(which == d, rolled[d - i], out)
                dst[GX + g * tx + i, pl.ds(GY + y, 8), :] = out

    each_x(0, ng, 1, gather)
    each_x(0, ng, 1, body)


def add_refined(L, src, dst, E, ex, ey, k):
    half = (L.yhi - L.ylo) // 2

    def body(x, i):
        for p in range(2):
            e = E[ex + 2 * i + p, pl.ds(ey, half), :]
            for dx in range(2):
                for phase in range(2):
                    at = (x + 2 * p + dx, pl.ds(L.ylo + phase, half, stride=2), slice(None))
                    yield dst, at, src[at] + e

    each_group(L.x0 - k, L.nx + 2 * k, 4, half // 4, body)


def total_of(values):
    return jnp.sum(values, axis=(0, 1, 2), keepdims=True)


def krylov(L, F, E, V):
    at = (pl.ds(L.x0, L.nx), pl.ds(L.y0, L.ny), slice(None))
    remain = F[at]
    direction = remain
    values = jnp.zeros_like(remain)
    norm_now = total_of(remain * remain)
    for step in range(NB):
        V[at] = direction
        _, total = off_diagonal(L, V, L.x0, L.nx, L.y0, L.ny)
        image = L.D[pl.ds(L.x0, L.nx)] * direction - total
        alpha = norm_now / total_of(direction * image)
        values = values + alpha * direction
        if step < NB - 1:
            remain = remain - alpha * image
            norm_next = total_of(remain * remain)
            direction = remain + (norm_next / norm_now) * direction
            norm_now = norm_next
    E[at] = values


def zero(ref):
    def body(i, _):
        ref[i] = jnp.zeros(ref.shape[1:], ref.dtype)

    each_x(0, ref.shape[0], 1, body)


def zero_halo(ref, L, k, edges):
    y0, y1, nx = L.y0, L.y0 + L.ny, L.nx

    def ends(start):
        for i in range(k):
            ref[start + i, pl.ds(y0 - 8, L.ny + 16), :] = jnp.zeros((L.ny + 16, LANES), ref.dtype)

    def side(y):
        def rows(x, _):
            ref[pl.ds(x, 8), pl.ds(y, 8), :] = jnp.zeros((8, 8, LANES), ref.dtype)

        each_x(0, ref.shape[0], 8, rows)

    first_x, last_x, first_y, last_y = edges
    pl.when(first_x)(lambda: ends(HX - k))
    pl.when(last_x)(lambda: ends(HX + nx))
    pl.when(first_y)(lambda: side(y0 - 8))
    pl.when(last_y)(lambda: side(y1))


def kernel(ng, nb, source, tags, coef, rough, out_v, out_r, *scratch):
    scratch = list(scratch)

    def take(count):
        taken = scratch[:count]
        del scratch[:count]
        return taken

    g, b = lax.axis_index("grp"), lax.axis_index("box")
    me = g * nb + b
    count = ng * nb
    none = lax.div(g, jnp.int32(ng))

    nx, ny = source.shape[0], source.shape[1]
    L = []
    for l in range(3):
        L.append(Level(1 << l, nx >> l, ny >> l, HX, YO, 8, (ny >> l) + 24, 4, none, take(8)))
    tx, ty = nx >> 3, ny >> 3
    L.append(Level(8, ng * tx, nb * ty, GX, GY, GY, GY + nb * ty, 4 if nb * ty <= 32 else 2, none, take(7)))
    L.append(Level(16, ng * tx // 2, nb * ty // 2, 2, GY, GY, GY + nb * ty // 2, ng * tx // 2, none, take(7)))
    f0, f1a, f1b, f2a, f2b, f3, f4, kept = take(8)
    f1, f2 = (f1a, f1b), (f2a, f2b)
    R0, R3 = take(2)
    R1 = R2 = R0
    flat = R3
    slots = take(3)
    halo_send, halo_recv, all_send, all_recv = take(4)

    edges = (g == 0, g == ng - 1, b == 0, b == nb - 1)
    for ref, level in [(L[0].C, L[0]), (f0, L[0]), (L[1].C, L[1]), (L[2].C, L[2])]:
        zero_halo(ref, level, 7, edges)

    barrier = pltpu.get_barrier_semaphore()

    all_g = [g] + [lax.rem(g + i, ng) for i in range(1, ng)]
    all_b = [b] + [lax.rem(b + i, nb) for i in range(1, nb)]

    def others(body):
        for i in range(ng):
            for j in range(nb):
                if i or j:
                    body(all_g[i], all_b[j])

    others(lambda go, bo: pl.semaphore_signal(
        barrier, inc=1, device_id=(go, bo), device_id_type=pl.DeviceIdType.MESH))

    def halo_copies(ref, level, h, slot, src=None):
        for index, (dx, dy) in enumerate(DIRECTIONS):
            n, m = level.nx, level.ny
            sx, tx_, wx = {-1: (HX, HX + n, h), 0: (HX, HX, n), 1: (HX + n - h, HX - h, h)}[dx]
            sy, ty_, wy = {-1: (YO, YO + m, 8), 0: (YO, YO, m), 1: (YO + m - 8, YO - 8, 8)}[dy]
            to_g, to_b, from_g, from_b = g + dx, b + dy, g - dx, b - dy
            sends = (to_g >= 0) & (to_g < ng) & (to_b >= 0) & (to_b < nb)
            receives = (from_g >= 0) & (from_g < ng) & (from_b >= 0) & (from_b < nb)
            lead, side = (0, 0) if src is None else (HX, YO)
            copy = pltpu.make_async_remote_copy(
                src_ref=(ref if src is None else src).at[pl.ds(sx - lead, wx), pl.ds(sy - side, wy), :],
                dst_ref=ref.at[pl.ds(tx_, wx), pl.ds(ty_, wy), :],
                send_sem=halo_send.at[slot, index],
                recv_sem=halo_recv.at[slot, index],
                device_id=(to_g, to_b),
                device_id_type=pl.DeviceIdType.MESH,
            )
            yield sends, receives, copy

    def halo_start(*args):
        for sends, _, copy in halo_copies(*args):
            pl.when(sends)(copy.start)

    def halo_wait(*args):
        for _, receives, copy in halo_copies(*args):
            pl.when(receives)(copy.wait_recv)

    def halo_sent(*args):
        for sends, _, copy in halo_copies(*args):
            pl.when(sends)(copy.wait_send)

    def gather_start(which):
        mine = slots[which].at[me]

        def body(go, bo):
            pltpu.make_async_remote_copy(
                src_ref=mine,
                dst_ref=mine,
                send_sem=all_send.at[which],
                recv_sem=all_recv.at[which],
                device_id=(go, bo),
                device_id_type=pl.DeviceIdType.MESH,
            ).start()

        others(body)

    def gather_wait(which, sem):
        part = slots[which].at[pl.ds(0, count - 1)]
        pltpu.make_async_copy(part, part, sem.at[which]).wait()

    def fill(x, _):
        stores = []
        for dx in range(2):
            for y in tiles(0, ny):
                tag = tags[x + dx, pl.ds(y, 8), :]
                value = jnp.full(tag.shape, coef[0], jnp.float32)
                for region in range(1, coef.shape[0]):
                    value = jnp.where(tag == region, coef[region], value)
                at = (HX + x + dx, pl.ds(YO + y, 8), slice(None))
                stores.append((L[0].C, at, value * rough[x + dx, pl.ds(y, 8), :] * 0.5))
                stores.append((f0, at, source[x + dx, pl.ds(y, 8), :]))
        store_all(stores)

    for ref, level in [(f1a, L[1]), (f1b, L[1]), (f2a, L[2]), (f2b, L[2]), (kept, L[0])]:
        zero_halo(ref, level, 7, edges)
    each_x(0, nx, 2, fill)
    pl.semaphore_wait(barrier, count - 1)
    start = [(L[0].C, L[0], 7, 0), (f0, L[0], 6, 1, source), (L[1].C, L[1], 7, 2), (L[2].C, L[2], 7, 3)]
    halo_start(*start[0])
    halo_start(*start[1])
    for level in L[3:]:
        zero(level.VA)
        zero(level.VB)
    coef_pairs(L[0], R0)
    coarse_rows(L[0], R0, 0.125, L[1].C, HX, YO)
    coef_pairs(L[1], R1)
    coarse_rows(L[1], R1, 0.125, L[2].C, HX, YO)
    coef_pairs(L[2], R2)
    slots[0][me] = packed(L[2], R2, 0.125)
    halo_start(*start[2])
    halo_start(*start[3])
    gather_start(0)
    halo_wait(*start[0])
    operators(L[0], 6)
    halo_wait(*start[1])
    first_sweep(L[0], f0, L[0].VA, 6)
    sweep(L[0], f0, L[0].VA, L[0].VB, 5)
    sent = list(start)

    for cycle in range(2):
        wide = 6 if cycle == 0 else 4
        if cycle == 1:
            sweep(L[0], f0, L[0].VB, L[0].VA, 2)
            sweep(L[0], f0, L[0].VA, L[0].VB, 1)
        residual_pairs(L[0], f0, L[0].VB, R0)
        coarse_rows(L[0], R0, 0.5, f1[cycle], HX, YO)
        args = (f1[cycle], L[1], 6, 4 + cycle)
        halo_start(*args)
        sent.append(args)
        if cycle == 1:
            def keep(x, _):
                at = (x, pl.ds(YO, ny), slice(None))
                kept[at] = L[0].VB[at]

            each_x(HX, nx, 1, keep)
            kept_args = (kept, L[0], 3, 8)
            halo_start(*kept_args)
            sent.append(kept_args)
        if cycle == 0:
            halo_wait(*start[2])
            operators(L[1], 6)
        halo_wait(*args)
        first_sweep(L[1], f1[cycle], L[1].VA, 6)
        sweep(L[1], f1[cycle], L[1].VA, L[1].VB, 5)
        residual_pairs(L[1], f1[cycle], L[1].VB, R1)
        coarse_rows(L[1], R1, 0.5, f2[cycle], HX, YO)
        args = (f2[cycle], L[2], 6, 6 + cycle)
        halo_start(*args)
        sent.append(args)
        if cycle == 0:
            halo_wait(*start[3])
            operators(L[2], 6)
        halo_wait(*args)
        first_sweep(L[2], f2[cycle], L[2].VA, 6)
        sweep(L[2], f2[cycle], L[2].VA, L[2].VB, 5)
        residual_pairs(L[2], f2[cycle], L[2].VB, R2)
        slots[1 + cycle][me] = packed(L[2], R2, 0.5)
        gather_start(1 + cycle)
        if cycle == 0:
            gather_wait(0, all_recv)
            unpack(slots[0], flat, L[3].C, ng, nb, tx, ty)
            operators(L[3], 0)
            coef_pairs(L[3], R3)
            coarse_rows(L[3], R3, 0.125, L[4].C, 2, GY)
            operators(L[4], 0)
        gather_wait(1 + cycle, all_recv)
        unpack(slots[1 + cycle], flat, f3, ng, nb, tx, ty)
        first_sweep(L[3], f3, L[3].VA, 0)
        sweep(L[3], f3, L[3].VA, L[3].VB, 0)
        residual_pairs(L[3], f3, L[3].VB, R3)
        coarse_rows(L[3], R3, 0.5, f4, 2, GY)
        krylov(L[4], f4, L[4].VB, L[4].VA)
        add_refined(L[3], L[3].VB, L[3].VB, L[4].VB, 2, GY, 0)
        sweep(L[3], f3, L[3].VB, L[3].VA, 0)
        sweep(L[3], f3, L[3].VA, L[3].VB, 0)
        add_refined(L[2], L[2].VB, L[2].VB, L[3].VB, GX + g * tx - wide // 2,
                    pl.multiple_of(GY - 4 + b * ty, 4), wide)
        sweep(L[2], f2[cycle], L[2].VB, L[2].VA, wide // 2 + 1)
        sweep(L[2], f2[cycle], L[2].VA, L[2].VB, wide // 2)
        add_refined(L[1], L[1].VB, L[1].VB, L[2].VB, HX - wide // 2, YO - 4, wide)
        sweep(L[1], f1[cycle], L[1].VB, L[1].VA, wide // 2 + 1)
        sweep(L[1], f1[cycle], L[1].VA, L[1].VB, wide // 2)
        if cycle == 1:
            halo_wait(*kept_args)
        before = L[0].VB if cycle == 0 else kept
        add_refined(L[0], before, L[0].VB, L[1].VB, HX - wide // 2, YO - 4, wide)
        sweep(L[0], f0, L[0].VB, L[0].VA, wide - 2)
        sweep(L[0], f0, L[0].VA, L[0].VB, wide - 3)

    def finish(x, i):
        for y in tiles(YO, YO + ny):
            at = (pl.ds(x, 2), pl.ds(y, 8), slice(None))
            to = (pl.ds(2 * i, 2), pl.ds(y - YO, 8), slice(None))
            center, total = off_diagonal(L[0], L[0].VB, x, 2, y, 8)
            out_v[to] = center
            out_r[to] = f0[at] - L[0].D[pl.ds(x, 2), pl.ds(y - YO, 8), :] * center + total

    each_x(HX, nx, 2, finish)
    for args in sent:
        halo_sent(*args)
    for which in range(3):
        gather_wait(which, all_send)


def body(ng, nb, source_field, region_tags, region_coef, roughness):
    nx, ny, nz = source_field.shape
    f32 = jnp.float32
    shapes = []
    padded = [(((nx >> l) + 2 * HX, (ny >> l) + 2 * YO, nz)) for l in range(3)]
    tx, ty = nx >> 3, ny >> 3
    padded.append((ng * tx + 2 * GX, nb * ty + 2 * GY, nz))
    padded.append((ng * tx // 2 + 4, nb * ty // 2 + 2 * GY, nz))
    for index, shape in enumerate(padded):
        own = (shape[0], shape[1] - 2 * (YO if index < 3 else GY), nz)
        shapes += [shape] * 4 + [own] + [shape] * (3 if index < 3 else 2)
    shapes += [padded[0], padded[1], padded[1], padded[2], padded[2], padded[3], padded[4], padded[0]]
    shapes += [(nx // 2, ny, nz), (ng * tx // 2, nb * ty, nz)]
    shapes += [(ng * nb, ty, nz)] * 3
    dma = pltpu.SemaphoreType.DMA
    vmem = pl.BlockSpec(memory_space=pltpu.VMEM)
    return pl.pallas_call(
        functools.partial(kernel, ng, nb),
        out_shape=[jax.ShapeDtypeStruct(source_field.shape, f32)] * 2,
        in_specs=[vmem, vmem, pl.BlockSpec(memory_space=pltpu.SMEM), vmem],
        out_specs=[vmem, vmem],
        scratch_shapes=[pltpu.VMEM(shape, f32) for shape in shapes]
        + [dma((9, 8)), dma((9, 8)), dma((3,)), dma((3,))],
        compiler_params=pltpu.CompilerParams(
            collective_id=0, has_side_effects=True, vmem_limit_bytes=63 * 1024 * 1024
        ),
    )(source_field, region_tags, region_coef, roughness)


def solution(mesh):
    spec = P("grp", "box", None)
    return jax.shard_map(
        functools.partial(body, mesh.shape["grp"], mesh.shape["box"]),
        mesh=mesh,
        in_specs=(spec, spec, P(), spec),
        out_specs=(spec, spec),
        check_vma=False,
    )
```
